128 devices in a mesh: tm: 16 (over y_lo, z, core), space: 8 (over x, y_hi).
Axes of the slice: x: 4, y: 4 (y_hi: 2, y_lo: 2; y = y_hi * 2 + y_lo), z: 4, core: 2. Of those that a mesh axis runs over, the one named last changes fastest.
Arguments:
- initial_temp: float32 [128, 32, 256], P('space'), may hold values from -6 to 6
- region_labels: int32 [32, 8, 64], P('space'), may hold values from 0 to 5
- region_rate: float32 [6], replicated, may hold values from 0.5 to 8
- heat_rate: float32 [16, 6], replicated, may hold values from 0.1 to 2
Outputs:
- slice_end: float32 [16, 128, 32, 256], P('tm', 'space')
The draws below stay inside these ranges and needn't reach their ends.
All inputs are finite; a program needn't handle non-finite values.
Results may differ from the reference program's by a relative error of at most 0.0001.
Values sent between devices are 32-bit elements; how exact they have to be, the bound alone decides.
No kernel may reach another device: no remote copies, remote signals or barrier semaphores. Data moves between devices by JAX's collectives and lax.ppermute only.
A program may use at most 128 MiB of HBM per device.

```python
import math
import jax
import jax.numpy as jnp
from jax import lax

NY = 32
NZ = 256
FINE_STEPS = 2
SWEEPS = 8
C_SWEEPS = 4
PARA_ITERS = 2
REGIONS = 6
SLICES = 16
NX = 128


def with_ends(drawn, key, least, top_value):
    longest = drawn.shape.index(max(drawn.shape))
    spots = []
    for shift in (0, 1):
        where = [jax.random.randint(jax.random.fold_in(key, axis), (), 0, length) for axis, length in enumerate(drawn.shape)]
        where[longest] = (where[longest] + shift) % drawn.shape[longest]
        spots.append(tuple(where))
    return drawn.at[spots[0]].set(least).at[spots[1]].set(top_value)


def level_of(stream_key, extent, cuts, smallest, top_value):
    factor_of = 1.0
    for axis_at, shards_of in cuts:
        steps = jax.random.uniform(jax.random.fold_in(jax.random.fold_in(stream_key, 6), axis_at), (shards_of,), jnp.float32, smallest / len(cuts), top_value / len(cuts))
        factor_of = factor_of * jnp.repeat(jnp.exp(steps), extent[axis_at] // shards_of).reshape((-1,) + (1,) * (len(extent) - 1 - axis_at))
    return factor_of


def scatter_about(stream_key, shape, width, reach, shards=(), held_as=jnp.bfloat16):
    gain = level_of(stream_key, shape, shards, -0.22, 0.18) if shards else 1.0
    drawn = jax.random.normal(stream_key, shape, jnp.float32) * width * gain
    return jnp.minimum(jnp.maximum(drawn, -reach), reach).astype(held_as)


def setup_inputs(seed: int = 0) -> dict:
    seeds = jax.random.split(jax.random.key(seed), 5)
    return {
        "initial_temp": scatter_about(seeds[0], (NX, NY, NZ), 1.0, 6.0, ((0, 8),), jnp.float32),
        "region_labels": with_ends(jax.random.randint(seeds[1], (NX // 4, NY // 4, NZ // 4), 0, REGIONS), jax.random.fold_in(seeds[1], 1), 0, REGIONS - 1).astype(jnp.int32),
        "region_rate": jnp.clip(jnp.exp(jax.random.uniform(seeds[2], (REGIONS,), jnp.float32, math.log(0.5), math.log(8.0))), 0.5, 8.0),
        "heat_rate": jnp.clip(jax.random.uniform(seeds[3], (SLICES, REGIONS), jnp.float32, 0.1, 2.0), 0.1, 2.0),
    }


def neighbours(field):
    padded = jnp.pad(field, 1)
    total = padded[2:, 1:-1, 1:-1] + padded[:-2, 1:-1, 1:-1]
    total = total + padded[1:-1, 2:, 1:-1] + padded[1:-1, :-2, 1:-1]
    total = total + padded[1:-1, 1:-1, 2:] + padded[1:-1, 1:-1, :-2]
    return total


def expand(block):
    lead = block.shape[:-3]
    sx, sy, sz = block.shape[-3:]
    wide = jnp.broadcast_to(block[..., :, None, :, None, :, None], lead + (sx, 4, sy, 4, sz, 4))
    return wide.reshape(lead + (4 * sx, 4 * sy, 4 * sz))


def restrict(field):
    lead = field.shape[:-3]
    sx, sy, sz = field.shape[-3:]
    split = field.reshape(lead + (sx // 4, 4, sy // 4, 4, sz // 4, 4))
    return jnp.mean(split, axis=(-5, -3, -1))


def propagate(state, inverse, weight, source, count, sweeps):
    for outer_index in range(count):
        scaled = (state + source) * inverse
        field = state
        for sweep_index in range(sweeps):
            field = scaled + weight * neighbours(field)
        state = field
    return state


def reference(initial_temp, region_labels, region_rate, heat_rate):
    rate = region_rate[region_labels]
    rate_fine = expand(rate)
    inv_fine = 1.0 / (1.0 + 6.0 * rate_fine)
    weight_fine = rate_fine * inv_fine
    rate_coarse = FINE_STEPS * rate / 16.0
    inv_coarse = 1.0 / (1.0 + 6.0 * rate_coarse)
    weight_coarse = rate_coarse * inv_coarse

    def fine_one(state, row):
        return propagate(state, inv_fine, weight_fine, expand(row[region_labels]), FINE_STEPS, SWEEPS)

    def coarse_one(coarse, row):
        return propagate(coarse, inv_coarse, weight_coarse, FINE_STEPS * row[region_labels], 1, C_SWEEPS)

    start = restrict(initial_temp)

    def chain(deltas):
        def advance(coarse, pair):
            row, delta = pair
            return coarse_one(coarse, row) + delta, coarse

        unused, starts = lax.scan(advance, start, (heat_rate, deltas))
        return starts, jax.vmap(coarse_one)(starts, heat_rate)

    starts, ends = chain(jnp.zeros((SLICES,) + start.shape, jnp.float32))
    states = jnp.concatenate([initial_temp[None], expand(starts[1:])], axis=0)
    corrected = states
    for iteration in range(PARA_ITERS):
        fine_ends = jax.vmap(fine_one)(states, heat_rate)
        starts, new_ends = chain(restrict(fine_ends) - ends)
        corrected = fine_ends + expand(new_ends - ends)
        ends = new_ends
        states = jnp.concatenate([initial_temp[None], corrected[:-1]], axis=0)
    return corrected
```

```python
import jax
import jax.numpy as jnp
from jax import lax
from jax.experimental import pallas as pl
from jax.experimental.pallas import tpu as pltpu
from jax.sharding import PartitionSpec as P


FINE_STEPS = 2
SWEEPS = 8
C_SWEEPS = 4
WINDOW = 40
NEAR = 16
OWN = 32
GROUPS = WINDOW // 4
VMEM = 48 * 1024 * 1024

f32 = jnp.float32


def lane_of():
    return lax.broadcasted_iota(jnp.int32, (8, 128), 1)


def half_mask():
    return lane_of() < 64


def edge_masks():
    lane = lane_of()
    column = lax.rem(lane, 64)
    row = lax.broadcasted_iota(jnp.int32, (8, 128), 0)
    return row == 0, row == 7, column == 0, column == 63


def swap(tile):
    return pltpu.roll(tile, 64, 1)


def row_up(tile, masks):
    return jnp.where(masks[0], 0.0, pltpu.roll(tile, 1, 0))


def row_down(tile, masks):
    return jnp.where(masks[1], 0.0, pltpu.roll(tile, 7, 0))


def lane_up(tile, masks):
    return jnp.where(masks[2], 0.0, pltpu.roll(tile, 1, 1))


def lane_down(tile, masks):
    return jnp.where(masks[3], 0.0, pltpu.roll(tile, 127, 1))


def sweep(source, target, scaled, weight_ref, first, masks):
    def body(i, carry):
        weight = weight_ref[lax.shift_right_logical(i, 2)]
        cur = [source[i, p] for p in range(16)]
        for p in range(16):
            yi, zi = p // 4, p % 4
            total = source[i - 1, p] + source[i + 1, p]
            above = cur[p - 4] if yi > 0 else row_up(cur[p + 12], masks)
            below = cur[p + 4] if yi < 3 else row_down(cur[p - 12], masks)
            left = cur[p - 1] if zi > 0 else lane_up(cur[p + 3], masks)
            right = cur[p + 1] if zi < 3 else lane_down(cur[p - 3], masks)
            total = total + ((above + below) + (left + right))
            target[i, p] = scaled[i, p] + weight * total
        return carry

    lax.fori_loop(first, WINDOW, body, 0)
    fold(target)


def fold(buffer):
    for p in range(16):
        buffer[WINDOW, p] = swap(buffer[WINDOW - 1, p])


def propagate(even, odd, scaled, inverse_ref, weight_ref, source_ref, first):
    masks = edge_masks()
    for step in range(FINE_STEPS):
        start = first + step * SWEEPS

        def prepare(i, carry):
            k = lax.shift_right_logical(i, 2)
            inverse, source = inverse_ref[k], source_ref[k]
            for p in range(16):
                scaled[i, p] = (even[i, p] + source) * inverse
            return carry

        lax.fori_loop(start, WINDOW, prepare, 0)

        def pair(j, carry):
            sweep(even, odd, scaled, weight_ref, start + 2 * j + 1, masks)
            sweep(odd, even, scaled, weight_ref, start + 2 * j + 2, masks)
            return carry

        lax.fori_loop(0, SWEEPS // 2, pair, 0)


def fill(buffer, tiles_ref, first):
    def body(i, carry):
        tile = tiles_ref[lax.shift_right_logical(i, 2)]
        for p in range(16):
            buffer[i, p] = tile
        return carry

    lax.fori_loop(first, WINDOW, body, 0)
    fold(buffer)


def fill_blocks(buffer, own, left, right):
    half = half_mask()

    def body(j, carry):
        for p in range(16):
            buffer[NEAR + j, p] = jnp.where(half, left[j, p], right[j, p])
            buffer[NEAR + 15 - j, p] = swap(jnp.where(half, right[j, p], left[j, p]))
            buffer[OWN + j, p] = own[j, p]
        return carry

    lax.fori_loop(0, 8, body, 0)
    fold(buffer)


def restrict_own(buffer):
    tiles = []
    for k in range(2):
        total = None
        for i in range(4):
            for p in range(16):
                tile = buffer[OWN + 4 * k + i, p]
                total = tile if total is None else total + tile
        tiles.append(total * (1.0 / 64.0))
    return tiles


def coarse_sweep(field, scaled, weight, masks):
    result = []
    for i in range(16):
        here = field[i]
        beyond = field[i + 1] if i < 15 else swap(here)
        total = (row_up(here, masks) + row_down(here, masks)) + (
            lane_up(here, masks) + lane_down(here, masks)
        )
        total = total + (beyond + field[i - 1] if i > 0 else beyond)
        result.append(scaled[i] + weight[i] * total)
    return result


def blocks_to_global(load, half):
    tiles = []
    for i in range(16):
        block, place = i // 4, i % 4
        if place < 2:
            tiles.append(jnp.where(half, load(block, place), load(7 - block, place)))
        else:
            tiles.append(
                swap(jnp.where(half, load(7 - block, 3 - place), load(block, 3 - place)))
            )
    return tiles


def spread(padded, tiles, half):
    for i in range(16):
        other = swap(tiles[i])
        padded[8 + i] = jnp.where(half, tiles[i], other)
        padded[39 - i] = jnp.where(half, other, tiles[i])


def window_tile(padded, space, k, half):
    return jnp.where(half, padded[4 * space + k], padded[4 * space + 19 - k])


def difference_chain(received, shift, table_ref, ends, masks, half):
    def body(m, delta):
        scaled = [delta[i] * table_ref[0, i] for i in range(16)]
        weight = [table_ref[1, i] for i in range(16)]
        field = list(delta)
        for _ in range(C_SWEEPS):
            field = coarse_sweep(field, scaled, weight, masks)
        for i in range(16):
            ends[m, i] = field[i]
        sender = jnp.minimum(m + shift, 15)
        added = blocks_to_global(lambda b, k: received[sender * 8 + b, k], half)
        return tuple(field[i] + added[i] for i in range(16))

    zero = jnp.zeros((8, 128), f32)
    lax.fori_loop(0, 16, body, (zero,) * 16)


def split_dot(values, matrix):
    high = values.astype(jnp.bfloat16)
    rest = values - high.astype(f32)
    middle = rest.astype(jnp.bfloat16)
    low = (rest - middle.astype(f32)).astype(jnp.bfloat16)

    def dot(part):
        return jnp.dot(part, matrix, preferred_element_type=f32)

    return dot(high) + (dot(middle) + dot(low))


def interleave_matrix(transposed):
    rows = lax.broadcasted_iota(jnp.int32, (256, 256), 0)
    columns = lax.broadcasted_iota(jnp.int32, (256, 256), 1)
    z, c = (columns, rows) if transposed else (rows, columns)
    hit = z == 4 * lax.rem(c, 64) + lax.div(c, 64)
    return jnp.where(hit, 1.0, 0.0).astype(jnp.bfloat16)


def to_phases(initial, labels, block, send, narrow, left, right):
    half = half_mask()
    matrix = interleave_matrix(False)
    for side in range(2):
        lanes = pl.ds(side * 128, 128)
        narrow[side] = initial[:, :, lanes].reshape(512, 128)
        for plane in range(16):
            for yi in range(4):
                rows = pl.ds(plane * 32 + yi, 8, stride=4)
                left[pl.ds(plane * 32 + yi * 8, 8), lanes] = narrow[side, rows, :]
    right[...] = split_dot(left[...], matrix)
    sums = []
    for k in range(2):
        total = jnp.zeros((8, 128), f32)
        for i in range(4 * k, 4 * k + 4):
            for yi in range(4):
                for pair in range(2):
                    lanes = pl.ds(pair * 128, 128)
                    a = right[pl.ds(i * 32 + yi * 8, 8), lanes]
                    b = right[pl.ds((15 - i) * 32 + yi * 8, 8), lanes]
                    even = jnp.where(half, a, swap(b))
                    odd = jnp.where(half, swap(a), b)
                    block[i, yi * 4 + 2 * pair] = even
                    block[i, yi * 4 + 2 * pair + 1] = odd
                    total = total + (even + odd)
        sums.append(total * (1.0 / 64.0))
    tags = [
        jnp.concatenate([labels[k], labels[3 - k]], axis=1).astype(f32) for k in range(2)
    ]
    for peer in range(8):
        for k in range(2):
            send[peer, k] = sums[k]
            send[peer, 2 + k] = tags[k]


def regions(tags, values):
    total = jnp.where(tags == 0.0, values[0], 0.0)
    for region in range(1, len(values)):
        total = jnp.where(tags == region, values[region], total)
    return total


def first_sweeps(
    place, rates, heat, received, block, left, right,
    send, end_block, base, fine, table, window,
    chain, padded, even, odd, scaled, local,
):
    half = half_mask()
    masks = edge_masks()
    index, space = place[0], place[1]
    before = jnp.maximum(index - 1, 0)
    count = 6
    rate_values = [rates[r] for r in range(count)]
    tags = blocks_to_global(lambda b, k: received[b, 2 + k], half)
    start = blocks_to_global(lambda b, k: received[b, k], half)
    for i in range(16):
        rate = FINE_STEPS * regions(tags[i], rate_values) / 16.0
        inverse = 1.0 / (1.0 + 6.0 * rate)
        table[0, i] = inverse
        table[1, i] = rate * inverse
        table[2, i] = tags[i]
        chain[0, i] = start[i]

    outside = jnp.full((8, 128), -1.0, f32)
    for i in range(8):
        padded[i] = outside
        padded[40 + i] = outside
    spread(padded, tags, half)
    for k in range(GROUPS):
        tag = window_tile(padded, space, k, half)
        rate = regions(tag, rate_values)
        inverse = jnp.where(tag < 0.0, 0.0, 1.0 / (1.0 + 6.0 * rate))
        fine[0, k] = inverse
        fine[1, k] = rate * inverse
        fine[2, k] = regions(tag, [heat[before, r] for r in range(count)])
        fine[3, k] = regions(tag, [heat[index, r] for r in range(count)])

    def advance(m, state):
        values = [FINE_STEPS * heat[m, r] for r in range(count)]
        weight = [table[1, i] for i in range(16)]
        rows = [
            (state[i] + regions(table[2, i], values)) * table[0, i] for i in range(16)
        ]
        field = list(state)
        for _ in range(C_SWEEPS):
            field = coarse_sweep(field, rows, weight, masks)
        for i in range(16):
            chain[m + 1, i] = field[i]
        return tuple(field)

    lax.fori_loop(0, 16, advance, tuple(start))

    nothing = jnp.zeros((8, 128), f32)
    for i in range(8):
        padded[i] = nothing
        padded[40 + i] = nothing
    spread(padded, [chain[before + 1, i] for i in range(16)], half)
    before_end = [window_tile(padded, space, 8 + k, half) for k in range(2)]
    spread(padded, [chain[index + 1, i] for i in range(16)], half)
    for k in range(2):
        base[k] = window_tile(padded, space, 8 + k, half)
    spread(padded, [chain[before, i] for i in range(16)], half)
    for k in range(GROUPS):
        window[k] = window_tile(padded, space, k, half)

    for k in range(3):
        local[k] = fine[k]

    @pl.when(index >= 2)
    def _():
        fill(even, window, NEAR)

    @pl.when(index < 2)
    def _():
        fill_blocks(even, block, left, right)

    propagate(even, odd, scaled, local.at[0], local.at[1], local.at[2], NEAR)
    means = restrict_own(even)
    for k in range(2):
        delta = means[k] - before_end[k]

        def put(peer, carry):
            send[peer, k] = delta
            return carry

        lax.fori_loop(0, 128, put, 0)

    @pl.when(index == 0)
    def _():
        end_block[...] = block[...]

    @pl.when(index > 0)
    def _():
        end_block[...] = even[pl.ds(OWN, 8)]


def wide_sweeps(place, fine, window, state, even, odd, scaled):
    @pl.when(place[0] >= 2)
    def _():
        fill(even, window, 0)
        propagate(even, odd, scaled, fine.at[0], fine.at[1], fine.at[2], 0)
        state[...] = even[pl.ds(NEAR, WINDOW - NEAR)]


def second_sweeps(
    place, received, state, end_block, left, right, base, fine, table,
    send, result,
    ends, padded, even, odd, scaled, window,
):
    half = half_mask()
    masks = edge_masks()
    index, space = place[0], place[1]
    before = jnp.maximum(index - 1, 0)
    difference_chain(received, 1, table, ends, masks, half)

    nothing = jnp.zeros((8, 128), f32)
    for i in range(8):
        padded[i] = nothing
        padded[40 + i] = nothing
    spread(padded, [ends[index, i] for i in range(16)], half)
    own_end = [window_tile(padded, space, 8 + k, half) + base[k] for k in range(2)]
    spread(padded, [ends[before, i] for i in range(16)], half)
    keep = jnp.where(index > 0, 1.0, 0.0)
    for k in range(GROUPS):
        window[k] = window_tile(padded, space, k, half) * keep

    @pl.when(index >= 2)
    def _():
        even[pl.ds(NEAR, WINDOW - NEAR)] = state[...]

    @pl.when(index < 2)
    def _():
        fill_blocks(even, end_block, left, right)

    def correct(i, carry):
        tile = window[lax.shift_right_logical(i, 2)]
        for p in range(16):
            even[i, p] = even[i, p] + tile
        return carry

    lax.fori_loop(NEAR, WINDOW, correct, 0)
    fold(even)
    propagate(even, odd, scaled, fine.at[0], fine.at[1], fine.at[3], NEAR)
    result[...] = even[pl.ds(OWN, 8)]
    means = restrict_own(even)
    after = jnp.minimum(index + 1, 15) * 8 + space
    for k in range(2):
        change = (means[k] - own_end[k]) - received[after, k]

        def put(peer, carry):
            send[peer, k] = change
            return carry

        lax.fori_loop(0, 128, put, 0)


def finish(place, received, field, table, out, ends, padded, narrow, left, right):
    half = half_mask()
    masks = edge_masks()
    index, space = place[0], place[1]
    difference_chain(received, 0, table, ends, masks, half)
    spread(padded, [ends[index, i] for i in range(16)], half)
    matrix = interleave_matrix(True)
    for k in range(2):
        tile = window_tile(padded, space, 8 + k, half)
        for i in range(4 * k, 4 * k + 4):
            for yi in range(4):
                for pair in range(2):
                    p = yi * 4 + 2 * pair
                    even, odd = field[i, p] + tile, field[i, p + 1] + tile
                    lanes = pl.ds(pair * 128, 128)
                    left[pl.ds(i * 32 + yi * 8, 8), lanes] = jnp.where(half, even, swap(odd))
                    left[pl.ds((15 - i) * 32 + yi * 8, 8), lanes] = jnp.where(
                        half, swap(even), odd
                    )
    right[...] = split_dot(left[...], matrix)
    for side in range(2):
        lanes = pl.ds(side * 128, 128)
        for plane in range(16):
            for yi in range(4):
                rows = pl.ds(plane * 32 + yi, 8, stride=4)
                narrow[side, rows, :] = right[pl.ds(plane * 32 + yi * 8, 8), lanes]
        out[0, :, :, lanes] = narrow[side].reshape(16, 32, 128)


def call(kernel, operands, results, scratch, scalars=1, flops=0):
    specs = [pl.BlockSpec(memory_space=pltpu.SMEM)] * scalars
    specs += [pl.BlockSpec(memory_space=pltpu.VMEM)] * (len(operands) - scalars)
    shapes = [jax.ShapeDtypeStruct(shape, f32) for shape in results]
    out_specs = [pl.BlockSpec(memory_space=pltpu.VMEM)] * len(results)
    moved = sum(4 * x.size for x in operands) + sum(4 * x.size for x in shapes)
    return pl.pallas_call(
        kernel,
        out_shape=shapes,
        in_specs=specs,
        out_specs=out_specs,
        scratch_shapes=[pltpu.VMEM(shape, f32) for shape in scratch],
        compiler_params=pltpu.CompilerParams(vmem_limit_bytes=VMEM),
        cost_estimate=pl.CostEstimate(flops=flops, bytes_accessed=moved, transcendentals=0),
        name=kernel.__name__,
    )(*operands)


def on_device(initial_temp, region_labels, region_rate, heat_rate):
    peers = lax.axis_size("space")
    index, space = lax.axis_index("tm"), lax.axis_index("space")
    place = jnp.stack([index, space]).astype(jnp.int32)
    tile = (8, 128)
    block_shape = (8, 16) + tile
    wide_shape = (WINDOW + 1, 16) + tile

    block, send = call(
        to_phases, (initial_temp, region_labels),
        (block_shape, (8, 4) + tile), [(2, 512, 128), (512, 256), (512, 256)], scalars=0,
    )

    def beside(array, slices):
        def pairs(by):
            return [
                (t * peers + s, t * peers + s + by)
                for t in slices for s in range(peers) if 0 <= s + by < peers
            ]
        axes = ("tm", "space")
        return lax.ppermute(array, axes, pairs(1)), lax.ppermute(array, axes, pairs(-1))

    left, right = beside(block, (1,))
    received = lax.all_to_all(
        send.reshape(8 * 32, 128), "space", 0, 0, tiled=True
    ).reshape((8, 4) + tile)

    send, end_block, base, fine, table, window = call(
        first_sweeps,
        (place, region_rate, heat_rate, received, block, left, right),
        ((128, 2) + tile, block_shape, (2,) + tile, (4, GROUPS) + tile,
         (3, 16) + tile, (GROUPS,) + tile),
        [(17, 16) + tile, (48,) + tile, wide_shape, wide_shape, wide_shape, (3, GROUPS) + tile],
        scalars=3,
    )

    def gather(array):
        rows = array.reshape(128 * 16, 128)
        rows = lax.all_to_all(rows, ("tm", "space"), 0, 0, tiled=True)
        return rows.reshape((128, 2) + tile)

    received = gather(send)
    left, right = beside(end_block, (0, 1))
    (state,) = call(
        wide_sweeps, (place, fine, window), ((WINDOW - NEAR, 16) + tile,),
        [wide_shape] * 3, flops=10**8,
    )
    send, result = call(
        second_sweeps,
        (place, received, state, end_block, left, right, base, fine, table),
        ((128, 2) + tile, block_shape),
        [(16, 16) + tile, (48,) + tile, wide_shape, wide_shape, wide_shape, (GROUPS,) + tile],
    )
    received = gather(send)
    (out,) = call(
        finish, (place, received, result, table), ((1, 16, 32, 256),),
        [(16, 16) + tile, (48,) + tile, (2, 512, 128), (512, 256), (512, 256)],
    )
    return out


def solution(mesh):
    return jax.shard_map(
        on_device,
        mesh=mesh,
        in_specs=(P("space", None, None), P("space", None, None), P(), P()),
        out_specs=P("tm", "space", None, None),
        check_vma=False,
    )
```

```python
import jax
import jax.numpy as jnp
from jax import lax
from jax.experimental import pallas as pl
from jax.experimental.pallas import tpu as pltpu
from jax.sharding import PartitionSpec as P


FINE_STEPS = 2
SWEEPS = 8
C_SWEEPS = 4
WINDOW = 40
NEAR = 16
OWN = 32
GROUPS = WINDOW // 4
UNROLL = 8
VMEM = 24 * 1024 * 1024
WIDE_VMEM = 62 * 1024 * 1024

f32 = jnp.float32


def lane_of():
    return lax.broadcasted_iota(jnp.int32, (8, 128), 1)


def coordinates():
    return lax.axis_index("tm"), lax.axis_index("space")


def half_mask():
    return lane_of() < 64


def edge_masks():
    lane = lane_of()
    column = lax.rem(lane, 64)
    row = lax.broadcasted_iota(jnp.int32, (8, 128), 0)
    return row == 0, row == 7, column == 0, column == 63


def swap(tile):
    return pltpu.roll(tile, 64, 1)


def row_up(tile, masks):
    return jnp.where(masks[0], 0.0, pltpu.roll(tile, 1, 0))


def row_down(tile, masks):
    return jnp.where(masks[1], 0.0, pltpu.roll(tile, 7, 0))


def lane_up(tile, masks):
    return jnp.where(masks[2], 0.0, pltpu.roll(tile, 1, 1))


def lane_down(tile, masks):
    return jnp.where(masks[3], 0.0, pltpu.roll(tile, 127, 1))


def sweep(source, target, scaled, weight_ref, start, stop, masks, fresh=None):
    def body(t, carry):
        base = start + UNROLL * t
        for u in range(UNROLL):
            i = base + u + 1
            k = lax.shift_right_logical(base + u, 2)
            weight = weight_ref[k]
            if fresh is not None:
                inverse, heat = fresh[0][k], fresh[1][k]
            cur = [source[i, p] for p in range(16)]
            for p in range(16):
                yi, zi = p // 4, p % 4
                total = source[i - 1, p] + source[i + 1, p]
                above = cur[p - 4] if yi > 0 else row_up(cur[p + 12], masks)
                below = cur[p + 4] if yi < 3 else row_down(cur[p - 12], masks)
                left = cur[p - 1] if zi > 0 else lane_up(cur[p + 3], masks)
                right = cur[p + 1] if zi < 3 else lane_down(cur[p - 3], masks)
                total = total + ((above + below) + (left + right))
                if fresh is None:
                    term = scaled[i, p]
                else:
                    term = (cur[p] + heat) * inverse
                    scaled[i, p] = term
                target[i, p] = term + weight * total
        return carry

    lax.fori_loop(0, stop, body, 0)


def fold(buffer):
    for p in range(16):
        buffer[WINDOW + 1, p] = swap(buffer[WINDOW, p])


def run_sweeps(even, odd, scaled, inverse_ref, weight_ref, source_ref, first):
    masks = edge_masks()

    def one(source, target, q, fresh=None):
        group = lax.div(first + q, UNROLL)
        steps = WINDOW // UNROLL - group
        sweep(source, target, scaled, weight_ref, UNROLL * group, steps, masks, fresh)
        fold(target)

    fold(even)
    for step in range(FINE_STEPS):
        base = step * SWEEPS
        one(even, odd, jnp.int32(base + 1), (inverse_ref, source_ref))

        def pair(j, carry):
            one(odd, even, base + 2 * j + 2)
            one(even, odd, base + 2 * j + 3)
            return carry

        lax.fori_loop(0, SWEEPS // 2 - 1, pair, 0)
        one(odd, even, jnp.int32(base + SWEEPS))


def fill(buffer, tiles_ref, first, last):
    def body(k, carry):
        tile = tiles_ref[k]
        for u in range(4):
            for p in range(16):
                buffer[4 * k + u + 1, p] = tile
        return carry

    lax.fori_loop(first, last, body, 0)


def fill_sides(buffer, first, left, right):
    half = half_mask()

    def body(j, carry):
        for p in range(16):
            buffer[first + j + 1, p] = jnp.where(half, left[j, p], right[j, p])
            buffer[first + 16 - j, p] = swap(jnp.where(half, right[j, p], left[j, p]))
        return carry

    lax.fori_loop(0, 8, body, 0)


def restrict_own(buffer):
    tiles = []
    for k in range(2):
        parts = []
        for i in range(4):
            for p in range(16):
                tile = buffer[OWN + 4 * k + i + 1, p]
                if len(parts) < 8:
                    parts.append(tile)
                else:
                    parts[p % 8] = parts[p % 8] + tile
        while len(parts) > 1:
            parts = [parts[j] + parts[j + 1] for j in range(0, len(parts), 2)]
        tiles.append(parts[0] * (1.0 / 64.0))
    return tiles


def coarse_sweep(field, scaled, weight, masks):
    result = []
    for i in range(16):
        here = field[i]
        beyond = field[i + 1] if i < 15 else swap(here)
        total = (row_up(here, masks) + row_down(here, masks)) + (
            lane_up(here, masks) + lane_down(here, masks)
        )
        total = total + (beyond + field[i - 1] if i > 0 else beyond)
        result.append(scaled[i] + weight[i] * total)
    return result


def blocks_to_global(load, half):
    tiles = []
    for i in range(16):
        block, place = i // 4, i % 4
        if place < 2:
            tiles.append(jnp.where(half, load(block, place), load(7 - block, place)))
        else:
            tiles.append(
                swap(jnp.where(half, load(7 - block, 3 - place), load(block, 3 - place)))
            )
    return tiles


def spread(padded, tiles, half):
    for i in range(16):
        other = swap(tiles[i])
        padded[8 + i] = jnp.where(half, tiles[i], other)
        padded[39 - i] = jnp.where(half, other, tiles[i])


def window_tile(padded, space, k, half):
    return jnp.where(half, padded[4 * space + k], padded[4 * space + 19 - k])


def difference_chain(received, shift, table_ref, ends, masks, half):
    def body(m, delta):
        scaled = [delta[i] * table_ref[0, i] for i in range(16)]
        weight = [table_ref[1, i] for i in range(16)]
        field = list(delta)
        for _ in range(C_SWEEPS):
            field = coarse_sweep(field, scaled, weight, masks)
        for i in range(16):
            ends[m, i] = field[i]
        sender = jnp.minimum(m + shift, 15)
        added = blocks_to_global(lambda b, k: received[sender * 8 + b, k], half)
        return tuple(field[i] + added[i] for i in range(16))

    zero = jnp.zeros((8, 128), f32)
    lax.fori_loop(0, 16, body, (zero,) * 16)


def split_dot(values, matrix):
    high = values.astype(jnp.bfloat16)
    rest = values - high.astype(f32)
    middle = rest.astype(jnp.bfloat16)
    low = (rest - middle.astype(f32)).astype(jnp.bfloat16)

    def dot(part):
        return jnp.dot(part, matrix, preferred_element_type=f32)

    return dot(high) + (dot(middle) + dot(low))


def interleave_matrix(transposed):
    rows = lax.broadcasted_iota(jnp.int32, (256, 256), 0)
    columns = lax.broadcasted_iota(jnp.int32, (256, 256), 1)
    z, c = (columns, rows) if transposed else (rows, columns)
    hit = z == 4 * lax.rem(c, 64) + lax.div(c, 64)
    return jnp.where(hit, 1.0, 0.0).astype(jnp.bfloat16)


def to_phases(initial, labels, block, send, narrow, left, right):
    half = half_mask()
    matrix = interleave_matrix(False)
    for side in range(2):
        lanes = pl.ds(side * 128, 128)
        narrow[side] = initial[:, :, lanes].reshape(512, 128)
        for plane in range(16):
            for yi in range(4):
                rows = pl.ds(plane * 32 + yi, 8, stride=4)
                left[pl.ds(plane * 32 + yi * 8, 8), lanes] = narrow[side, rows, :]
    right[...] = split_dot(left[...], matrix)
    sums = []
    for k in range(2):
        total = jnp.zeros((8, 128), f32)
        for i in range(4 * k, 4 * k + 4):
            for yi in range(4):
                for pair in range(2):
                    lanes = pl.ds(pair * 128, 128)
                    a = right[pl.ds(i * 32 + yi * 8, 8), lanes]
                    b = right[pl.ds((15 - i) * 32 + yi * 8, 8), lanes]
                    even = jnp.where(half, a, swap(b))
                    odd = jnp.where(half, swap(a), b)
                    block[i, yi * 4 + 2 * pair] = even
                    block[i, yi * 4 + 2 * pair + 1] = odd
                    total = total + (even + odd)
        sums.append(total * (1.0 / 64.0))
    tags = [
        jnp.concatenate([labels[k], labels[3 - k]], axis=1).astype(f32) for k in range(2)
    ]
    for peer in range(8):
        for k in range(2):
            send[peer, k] = sums[k]
            send[peer, 2 + k] = tags[k]


def regions(tags, values):
    total = jnp.where(tags == 0.0, values[0], 0.0)
    for region in range(1, len(values)):
        total = jnp.where(tags == region, values[region], total)
    return total


def first_chain(rates, heat, received, base, fine, table, window, chain, padded):
    half = half_mask()
    masks = edge_masks()
    index, space = coordinates()
    before = jnp.maximum(index - 1, 0)
    count = 6
    rate_values = [rates[r] for r in range(count)]
    tags = blocks_to_global(lambda b, k: received[b, 2 + k], half)
    start = blocks_to_global(lambda b, k: received[b, k], half)
    for i in range(16):
        rate = FINE_STEPS * regions(tags[i], rate_values) / 16.0
        inverse = 1.0 / (1.0 + 6.0 * rate)
        table[0, i] = inverse
        table[1, i] = rate * inverse
        table[2, i] = tags[i]
        chain[0, i] = start[i]

    outside = jnp.full((8, 128), -1.0, f32)
    for i in range(8):
        padded[i] = outside
        padded[40 + i] = outside
    spread(padded, tags, half)
    for k in range(GROUPS):
        tag = window_tile(padded, space, k, half)
        rate = regions(tag, rate_values)
        inverse = jnp.where(tag < 0.0, 0.0, 1.0 / (1.0 + 6.0 * rate))
        fine[0, k] = inverse
        fine[1, k] = rate * inverse
        fine[2, k] = regions(tag, [heat[before, r] for r in range(count)])
        fine[3, k] = regions(tag, [heat[index, r] for r in range(count)])

    def advance(m, state):
        values = [FINE_STEPS * heat[m, r] for r in range(count)]
        weight = [table[1, i] for i in range(16)]
        rows = [
            (state[i] + regions(table[2, i], values)) * table[0, i] for i in range(16)
        ]
        field = list(state)
        for _ in range(C_SWEEPS):
            field = coarse_sweep(field, rows, weight, masks)
        for i in range(16):
            chain[m + 1, i] = field[i]
        return tuple(field)

    lax.fori_loop(0, 16, advance, tuple(start))

    nothing = jnp.zeros((8, 128), f32)
    for i in range(8):
        padded[i] = nothing
        padded[40 + i] = nothing
    spread(padded, [chain[before + 1, i] for i in range(16)], half)
    for k in range(2):
        base[k] = window_tile(padded, space, 8 + k, half)
    spread(padded, [chain[index + 1, i] for i in range(16)], half)
    for k in range(2):
        base[2 + k] = window_tile(padded, space, 8 + k, half)
    spread(padded, [chain[before, i] for i in range(16)], half)
    for k in range(GROUPS):
        window[k] = window_tile(padded, space, k, half)


def move(pairs, semaphores):
    copies = [
        pltpu.make_async_copy(source, target, semaphores.at[j])
        for j, (source, target) in enumerate(pairs)
    ]
    for copy in copies:
        copy.start()
    return copies


def move_now(pairs, semaphores):
    for copy in move(pairs, semaphores):
        copy.wait()


def first_sweeps(
    block, left, right, far_left, far_right, base, fine, window,
    send, even, odd, scaled, sides, semaphores,
):
    index, _ = coordinates()

    @pl.when(index >= 2)
    def _():
        fill(even, window, NEAR // 4, GROUPS)

    @pl.when(index < 2)
    def _():
        move_now(
            [(left, sides.at[0]), (right, sides.at[1]), (block, even.at[pl.ds(OWN + 1, 8)])],
            semaphores,
        )
        fill_sides(even, NEAR, sides.at[0], sides.at[1])

    run_sweeps(even, odd, scaled, fine.at[0], fine.at[1], fine.at[2], NEAR)
    means = restrict_own(even)
    for k in range(2):
        delta = means[k] - base[k]
        for peer in range(128):
            send[peer, k] = delta


def wide_sweeps(
    fine, window, block, left, right, far_left, far_right,
    state, even, odd, scaled, sides, semaphores,
):
    index, _ = coordinates()

    @pl.when(index < 2)
    def _():
        move_now(
            [(left, sides.at[0]), (right, sides.at[1]), (far_left, sides.at[2]),
             (far_right, sides.at[3]), (block, even.at[pl.ds(OWN + 1, 8)])],
            semaphores,
        )
        fill_sides(even, NEAR, sides.at[0], sides.at[1])
        fill_sides(even, 0, sides.at[2], sides.at[3])

    @pl.when(index >= 2)
    def _():
        fill(even, window, 0, GROUPS)

    @pl.when(index > 0)
    def _():
        run_sweeps(even, odd, scaled, fine.at[0], fine.at[1], fine.at[2], 0)

    move_now([(even.at[pl.ds(NEAR + 1, WINDOW - NEAR)], state)], semaphores.at[pl.ds(0, 1)])


def second_sweeps(
    received, state, base, fine, table,
    send, result,
    ends, padded, even, odd, scaled, window, semaphores,
):
    half = half_mask()
    masks = edge_masks()
    index, space = coordinates()
    (arrival,) = move([(state, even.at[pl.ds(NEAR + 1, WINDOW - NEAR)])], semaphores)
    before = jnp.maximum(index - 1, 0)
    difference_chain(received, 1, table, ends, masks, half)

    nothing = jnp.zeros((8, 128), f32)
    for i in range(8):
        padded[i] = nothing
        padded[40 + i] = nothing
    spread(padded, [ends[index, i] for i in range(16)], half)
    own_end = [window_tile(padded, space, 8 + k, half) + base[2 + k] for k in range(2)]
    spread(padded, [ends[before, i] for i in range(16)], half)
    keep = jnp.where(index > 0, 1.0, 0.0)
    for k in range(GROUPS):
        window[k] = window_tile(padded, space, k, half) * keep

    arrival.wait()

    def correct(k, carry):
        tile = window[k]
        for u in range(4):
            for p in range(16):
                even[4 * k + u + 1, p] = even[4 * k + u + 1, p] + tile
        return carry

    lax.fori_loop(NEAR // 4, GROUPS, correct, 0)
    run_sweeps(even, odd, scaled, fine.at[0], fine.at[1], fine.at[3], NEAR)
    (copy,) = move([(even.at[pl.ds(OWN + 1, 8)], result)], semaphores)
    means = restrict_own(even)
    after = jnp.minimum(index + 1, 15) * 8 + space
    changes = [(means[k] - own_end[k]) - received[after, k] for k in range(2)]
    for peer in range(128):
        for k in range(2):
            send[peer, k] = changes[k]
    copy.wait()


def finish(received, result, table, out, ends, padded, narrow, left, right, field, semaphores):
    half = half_mask()
    masks = edge_masks()
    index, space = coordinates()
    (copy,) = move([(result, field)], semaphores)
    difference_chain(received, 0, table, ends, masks, half)
    spread(padded, [ends[index, i] for i in range(16)], half)
    matrix = interleave_matrix(True)
    copy.wait()
    for k in range(2):
        tile = window_tile(padded, space, 8 + k, half)
        for i in range(4 * k, 4 * k + 4):
            for yi in range(4):
                for pair in range(2):
                    p = yi * 4 + 2 * pair
                    even, odd = field[i, p] + tile, field[i, p + 1] + tile
                    lanes = pl.ds(pair * 128, 128)
                    left[pl.ds(i * 32 + yi * 8, 8), lanes] = jnp.where(half, even, swap(odd))
                    left[pl.ds((15 - i) * 32 + yi * 8, 8), lanes] = jnp.where(
                        half, swap(even), odd
                    )
    right[...] = split_dot(left[...], matrix)
    for side in range(2):
        lanes = pl.ds(side * 128, 128)
        for plane in range(16):
            for yi in range(4):
                rows = pl.ds(plane * 32 + yi, 8, stride=4)
                narrow[side, rows, :] = right[pl.ds(plane * 32 + yi * 8, 8), lanes]
        out[0, :, :, lanes] = narrow[side].reshape(16, 32, 128)


def call(kernel, operands, results, scratch, copies=0, flops=0, vmem=VMEM):
    where = {
        "scalar": pltpu.SMEM, "near": pltpu.VMEM, "far": pltpu.HBM,
    }
    shapes = [jax.ShapeDtypeStruct(shape, f32) for shape, _ in results]
    arrays = [x for x, _ in operands]
    moved = sum(4 * x.size for x in arrays) + sum(4 * x.size for x in shapes)
    semaphores = [pltpu.SemaphoreType.DMA((copies,))] if copies else []
    return pl.pallas_call(
        kernel,
        out_shape=shapes,
        in_specs=[pl.BlockSpec(memory_space=where[w]) for _, w in operands],
        out_specs=[pl.BlockSpec(memory_space=where[w]) for _, w in results],
        scratch_shapes=[pltpu.VMEM(shape, f32) for shape in scratch] + semaphores,
        compiler_params=pltpu.CompilerParams(vmem_limit_bytes=vmem),
        cost_estimate=pl.CostEstimate(flops=flops, bytes_accessed=moved, transcendentals=0),
        name=kernel.__name__,
    )(*arrays)


def on_device(initial_temp, region_labels, region_rate, heat_rate):
    peers = lax.axis_size("space")
    tile = (8, 128)
    block_shape = (8, 16) + tile
    buffer = (WINDOW + 2, 16) + tile

    block, send = call(
        to_phases,
        [(initial_temp, "near"), (region_labels, "near")],
        [(block_shape, "near"), ((8, 4) + tile, "near")],
        [(2, 512, 128), (512, 256), (512, 256)],
    )

    def beside(by, routes):
        pairs = [
            (t * peers + s + by, to * peers + s)
            for t, to in routes for s in range(peers) if 0 <= s + by < peers
        ]
        return lax.ppermute(block, ("tm", "space"), pairs)

    sides = [
        (beside(-1, ((8, 1), (10, 0))), "far"), (beside(1, ((9, 1), (11, 0))), "far"),
        (beside(-2, ((2, 1),)), "far"), (beside(2, ((6, 1),)), "far"),
    ]
    received = lax.all_to_all(
        send.reshape(8 * 32, 128), "space", 0, 0, tiled=True
    ).reshape((8, 4) + tile)

    base, fine, table, window = call(
        first_chain,
        [(region_rate, "scalar"), (heat_rate, "scalar"), (received, "near")],
        [((4,) + tile, "near"), ((4, GROUPS) + tile, "near"), ((3, 16) + tile, "near"),
         ((GROUPS,) + tile, "near")],
        [(17, 16) + tile, (48,) + tile],
    )
    base, fine, table, window = ((x, "near") for x in (base, fine, table, window))
    (send,) = call(
        first_sweeps,
        [(block, "far"), *sides, base, fine, window],
        [((128, 2) + tile, "near")],
        [buffer, buffer, buffer, (2,) + block_shape],
        copies=3,
    )

    def gather(array):
        rows = array.reshape(128 * 16, 128)
        rows = lax.all_to_all(rows, ("tm", "space"), 0, 0, tiled=True)
        return (rows.reshape((128, 2) + tile), "near")

    received = gather(send)
    (state,) = call(
        wide_sweeps,
        [fine, window, (block, "far"), *sides],
        [((WINDOW - NEAR, 16) + tile, "far")],
        [buffer, buffer, buffer, (4,) + block_shape],
        copies=5, flops=10**8, vmem=WIDE_VMEM,
    )
    send, result = call(
        second_sweeps,
        [received, (state, "far"), base, fine, table],
        [((128, 2) + tile, "near"), (block_shape, "far")],
        [(16, 16) + tile, (48,) + tile, buffer, buffer, buffer, (GROUPS,) + tile],
        copies=1,
    )
    (out,) = call(
        finish,
        [gather(send), (result, "far"), table],
        [((1, 16, 32, 256), "near")],
        [(16, 16) + tile, (48,) + tile, (2, 512, 128), (512, 256), (512, 256), block_shape],
        copies=1,
    )
    return out


def solution(mesh):
    return jax.shard_map(
        on_device,
        mesh=mesh,
        in_specs=(P("space", None, None), P("space", None, None), P(), P()),
        out_specs=P("tm", "space", None, None),
        check_vma=False,
    )
```

```python
import jax
import jax.numpy as jnp
from jax import lax
from jax.experimental import pallas as pl
from jax.experimental.pallas import tpu as pltpu
from jax.sharding import PartitionSpec as P


FINE_STEPS = 2
SWEEPS = 8
C_SWEEPS = 4
REGIONS = 6
WINDOW = 40
NEAR = 16
OWN = 32
GROUPS = WINDOW // 4
UNROLL = 8
VMEM = 24 * 1024 * 1024
WIDE_VMEM = 62 * 1024 * 1024

f32 = jnp.float32


def lane_of():
    return lax.broadcasted_iota(jnp.int32, (8, 128), 1)


def coordinates():
    return lax.axis_index("tm"), lax.axis_index("space")


def half_mask():
    return lane_of() < 64


def edge_masks():
    lane = lane_of()
    column = lax.rem(lane, 64)
    row = lax.broadcasted_iota(jnp.int32, (8, 128), 0)
    return row == 0, row == 7, column == 0, column == 63


def swap(tile):
    return pltpu.roll(tile, 64, 1)


def row_up(tile, masks):
    return jnp.where(masks[0], 0.0, pltpu.roll(tile, 1, 0))


def row_down(tile, masks):
    return jnp.where(masks[1], 0.0, pltpu.roll(tile, 7, 0))


def lane_up(tile, masks):
    return jnp.where(masks[2], 0.0, pltpu.roll(tile, 1, 1))


def lane_down(tile, masks):
    return jnp.where(masks[3], 0.0, pltpu.roll(tile, 127, 1))


def sweep(source, target, scaled, weight_ref, group, masks, fresh=None):
    def planes(base, last):
        for u in range(UNROLL):
            i = base + u + 1
            k = lax.shift_right_logical(base + u, 2)
            weight = weight_ref[k]
            if fresh is not None:
                inverse, heat = fresh[0][k], fresh[1][k]
            cur = [source[i, p] for p in range(16)]
            for p in range(16):
                yi, zi = p // 4, p % 4
                total = source[i - 1, p] + source[i + 1, p]
                above = cur[p - 4] if yi > 0 else row_up(cur[p + 12], masks)
                below = cur[p + 4] if yi < 3 else row_down(cur[p - 12], masks)
                left = cur[p - 1] if zi > 0 else lane_up(cur[p + 3], masks)
                right = cur[p + 1] if zi < 3 else lane_down(cur[p - 3], masks)
                total = total + ((above + below) + (left + right))
                if fresh is None:
                    term = scaled[i, p]
                else:
                    term = (cur[p] + heat) * inverse
                    scaled[i, p] = term
                value = term + weight * total
                target[i, p] = value
                if last and u == UNROLL - 1:
                    target[WINDOW + 1, p] = swap(value)

    def body(t, carry):
        planes(UNROLL * t, False)
        return carry

    lax.fori_loop(group, WINDOW // UNROLL - 1, body, 0)
    planes(jnp.int32(WINDOW - UNROLL), True)


def fold(buffer):
    for p in range(16):
        buffer[WINDOW + 1, p] = swap(buffer[WINDOW, p])


def run_sweeps(even, odd, scaled, inverse_ref, weight_ref, source_ref, first):
    masks = edge_masks()

    def one(source, target, q, fresh=None):
        group = lax.div(first + q, UNROLL)
        sweep(source, target, scaled, weight_ref, group, masks, fresh)

    fold(even)
    for step in range(FINE_STEPS):
        base = step * SWEEPS
        one(even, odd, jnp.int32(base + 1), (inverse_ref, source_ref))

        def pair(j, carry):
            one(odd, even, base + 2 * j + 2)
            one(even, odd, base + 2 * j + 3)
            return carry

        lax.fori_loop(0, SWEEPS // 2 - 1, pair, 0)
        one(odd, even, jnp.int32(base + SWEEPS))


def fill(buffer, tiles_ref, first, last):
    def body(k, carry):
        tile = tiles_ref[k]
        for u in range(4):
            for p in range(16):
                buffer[4 * k + u + 1, p] = tile
        return carry

    lax.fori_loop(first, last, body, 0)


def fill_sides(buffer, first, left, right):
    half = half_mask()

    def body(j, carry):
        for p in range(16):
            buffer[first + j + 1, p] = jnp.where(half, left[j, p], right[j, p])
            buffer[first + 16 - j, p] = swap(jnp.where(half, right[j, p], left[j, p]))
        return carry

    lax.fori_loop(0, 8, body, 0)


def restrict_own(buffer):
    tiles = []
    for k in range(2):
        parts = []
        for i in range(4):
            for p in range(16):
                tile = buffer[OWN + 4 * k + i + 1, p]
                if len(parts) < 8:
                    parts.append(tile)
                else:
                    parts[p % 8] = parts[p % 8] + tile
        while len(parts) > 1:
            parts = [parts[j] + parts[j + 1] for j in range(0, len(parts), 2)]
        tiles.append(parts[0] * (1.0 / 64.0))
    return tiles


def coarse_sweep(field, scaled, weight, masks):
    result = []
    for i in range(16):
        here = field[i]
        beyond = field[i + 1] if i < 15 else swap(here)
        total = (row_up(here, masks) + row_down(here, masks)) + (
            lane_up(here, masks) + lane_down(here, masks)
        )
        total = total + (beyond + field[i - 1] if i > 0 else beyond)
        result.append(scaled[i] + weight[i] * total)
    return result


def blocks_to_global(load, half):
    tiles = []
    for i in range(16):
        block, place = i // 4, i % 4
        if place < 2:
            tiles.append(jnp.where(half, load(block, place), load(7 - block, place)))
        else:
            tiles.append(
                swap(jnp.where(half, load(7 - block, 3 - place), load(block, 3 - place)))
            )
    return tiles


def spread(padded, tiles, half):
    for i in range(16):
        other = swap(tiles[i])
        padded[8 + i] = jnp.where(half, tiles[i], other)
        padded[39 - i] = jnp.where(half, other, tiles[i])


def window_tile(padded, space, k, half):
    return jnp.where(half, padded[4 * space + k], padded[4 * space + 19 - k])


def difference_chain(received, shift, table_ref, ends, masks, half):
    def arrived(sender):
        return blocks_to_global(lambda b, k: received[sender * 8 + b, k], half)

    def body(m, delta):
        scaled = [delta[i] * table_ref[0, i] for i in range(16)]
        weight = [table_ref[1, i] for i in range(16)]
        field = list(delta)
        for _ in range(C_SWEEPS):
            field = coarse_sweep(field, scaled, weight, masks)
        for i in range(16):
            ends[m, i] = field[i]
        added = arrived(jnp.minimum(m + shift, 15))
        return tuple(field[i] + added[i] for i in range(16))

    for i in range(16):
        ends[0, i] = jnp.zeros((8, 128), f32)
    lax.fori_loop(1, 16, body, tuple(arrived(shift)))


def split_dot(values, matrix):
    high = values.astype(jnp.bfloat16)
    rest = values - high.astype(f32)
    middle = rest.astype(jnp.bfloat16)
    low = (rest - middle.astype(f32)).astype(jnp.bfloat16)

    def dot(part):
        return jnp.dot(part, matrix, preferred_element_type=f32)

    return dot(high) + (dot(middle) + dot(low))


def interleave_matrix(transposed):
    rows = lax.broadcasted_iota(jnp.int32, (256, 256), 0)
    columns = lax.broadcasted_iota(jnp.int32, (256, 256), 1)
    z, c = (columns, rows) if transposed else (rows, columns)
    hit = z == 4 * lax.rem(c, 64) + lax.div(c, 64)
    return jnp.where(hit, 1.0, 0.0).astype(jnp.bfloat16)


def to_phases(rates, heat, initial, labels, block, send, values, narrow, left, right):
    for region in range(REGIONS):
        values[region] = jnp.full((8, 128), rates[region], f32)
        for m in range(16):
            values[REGIONS * (m + 1) + region] = jnp.full((8, 128), heat[region, m], f32)
    half = half_mask()
    matrix = interleave_matrix(False)
    for side in range(2):
        lanes = pl.ds(side * 128, 128)
        narrow[side] = initial[:, :, lanes].reshape(512, 128)
        for plane in range(16):
            for yi in range(4):
                rows = pl.ds(plane * 32 + yi, 8, stride=4)
                left[pl.ds(plane * 32 + yi * 8, 8), lanes] = narrow[side, rows, :]
    right[...] = split_dot(left[...], matrix)
    sums = []
    for k in range(2):
        total = jnp.zeros((8, 128), f32)
        for i in range(4 * k, 4 * k + 4):
            for yi in range(4):
                for pair in range(2):
                    lanes = pl.ds(pair * 128, 128)
                    a = right[pl.ds(i * 32 + yi * 8, 8), lanes]
                    b = right[pl.ds((15 - i) * 32 + yi * 8, 8), lanes]
                    even = jnp.where(half, a, swap(b))
                    odd = jnp.where(half, swap(a), b)
                    block[i, yi * 4 + 2 * pair] = even
                    block[i, yi * 4 + 2 * pair + 1] = odd
                    total = total + (even + odd)
        sums.append(total * (1.0 / 64.0))
    tags = [
        jnp.concatenate([labels[k], labels[3 - k]], axis=1).astype(f32) for k in range(2)
    ]
    for peer in range(8):
        for k in range(2):
            send[peer, k] = sums[k]
            send[peer, 2 + k] = tags[k]


def regions(tags, values):
    total = jnp.where(tags == 0.0, values[0], 0.0)
    for region in range(1, len(values)):
        total = jnp.where(tags == region, values[region], total)
    return total


def first_chain(values, received, base, fine, table, window, chain, padded):
    half = half_mask()
    masks = edge_masks()
    index, space = coordinates()
    before = jnp.maximum(index - 1, 0)
    rate_values = [values[r] for r in range(REGIONS)]

    def heat_values(m):
        return [values[REGIONS * (m + 1) + r] for r in range(REGIONS)]

    tags = blocks_to_global(lambda b, k: received[b, 2 + k], half)
    start = blocks_to_global(lambda b, k: received[b, k], half)
    for i in range(16):
        rate = FINE_STEPS * regions(tags[i], rate_values) / 16.0
        inverse = 1.0 / (1.0 + 6.0 * rate)
        table[0, i] = inverse
        table[1, i] = rate * inverse
        table[2, i] = tags[i]
        chain[0, i] = start[i]

    outside = jnp.full((8, 128), -1.0, f32)
    for i in range(8):
        padded[i] = outside
        padded[40 + i] = outside
    spread(padded, tags, half)
    for k in range(GROUPS):
        tag = window_tile(padded, space, k, half)
        rate = regions(tag, rate_values)
        inverse = jnp.where(tag < 0.0, 0.0, 1.0 / (1.0 + 6.0 * rate))
        fine[0, k] = inverse
        fine[1, k] = rate * inverse
        fine[2, k] = regions(tag, heat_values(before))
        fine[3, k] = regions(tag, heat_values(index))

    def advance(m, state):
        heats = [FINE_STEPS * x for x in heat_values(m)]
        weight = [table[1, i] for i in range(16)]
        rows = [
            (state[i] + regions(table[2, i], heats)) * table[0, i] for i in range(16)
        ]
        field = list(state)
        for _ in range(C_SWEEPS):
            field = coarse_sweep(field, rows, weight, masks)
        for i in range(16):
            chain[m + 1, i] = field[i]
        return tuple(field)

    lax.fori_loop(0, 16, advance, tuple(start))

    nothing = jnp.zeros((8, 128), f32)
    for i in range(8):
        padded[i] = nothing
        padded[40 + i] = nothing
    spread(padded, [chain[before + 1, i] for i in range(16)], half)
    for k in range(2):
        base[k] = window_tile(padded, space, 8 + k, half)
    spread(padded, [chain[index + 1, i] for i in range(16)], half)
    for k in range(2):
        base[2 + k] = window_tile(padded, space, 8 + k, half)
    spread(padded, [chain[before, i] for i in range(16)], half)
    for k in range(GROUPS):
        window[k] = window_tile(padded, space, k, half)


def move(pairs, semaphores):
    copies = [
        pltpu.make_async_copy(source, target, semaphores.at[j])
        for j, (source, target) in enumerate(pairs)
    ]
    for copy in copies:
        copy.start()
    return copies


def move_now(pairs, semaphores):
    for copy in move(pairs, semaphores):
        copy.wait()


def first_sweeps(
    block, left, right, far_left, far_right, base, fine, window,
    send, even, odd, scaled, sides, semaphores,
):
    index, _ = coordinates()

    @pl.when(index >= 2)
    def _():
        fill(even, window, NEAR // 4, GROUPS)

    @pl.when(index < 2)
    def _():
        move_now(
            [(left, sides.at[0]), (right, sides.at[1]), (block, even.at[pl.ds(OWN + 1, 8)])],
            semaphores,
        )
        fill_sides(even, NEAR, sides.at[0], sides.at[1])

    run_sweeps(even, odd, scaled, fine.at[0], fine.at[1], fine.at[2], NEAR)
    means = restrict_own(even)
    for k in range(2):
        delta = means[k] - base[k]
        for peer in range(128):
            send[peer, k] = delta


def wide_sweeps(
    fine, window, block, left, right, far_left, far_right,
    state, even, odd, scaled, sides, semaphores,
):
    index, _ = coordinates()

    @pl.when(index < 2)
    def _():
        move_now(
            [(left, sides.at[0]), (right, sides.at[1]), (far_left, sides.at[2]),
             (far_right, sides.at[3]), (block, even.at[pl.ds(OWN + 1, 8)])],
            semaphores,
        )
        fill_sides(even, NEAR, sides.at[0], sides.at[1])
        fill_sides(even, 0, sides.at[2], sides.at[3])

    @pl.when(index >= 2)
    def _():
        fill(even, window, 0, GROUPS)

    @pl.when(index > 0)
    def _():
        run_sweeps(even, odd, scaled, fine.at[0], fine.at[1], fine.at[2], 0)

    move_now([(even.at[pl.ds(NEAR + 1, WINDOW - NEAR)], state)], semaphores.at[pl.ds(0, 1)])


def second_sweeps(
    received, state, base, fine, table,
    send, result,
    ends, padded, even, odd, scaled, window, semaphores,
):
    half = half_mask()
    masks = edge_masks()
    index, space = coordinates()
    (arrival,) = move([(state, even.at[pl.ds(NEAR + 1, WINDOW - NEAR)])], semaphores)
    before = jnp.maximum(index - 1, 0)
    difference_chain(received, 1, table, ends, masks, half)

    nothing = jnp.zeros((8, 128), f32)
    for i in range(8):
        padded[i] = nothing
        padded[40 + i] = nothing
    spread(padded, [ends[index, i] for i in range(16)], half)
    own_end = [window_tile(padded, space, 8 + k, half) + base[2 + k] for k in range(2)]
    spread(padded, [ends[before, i] for i in range(16)], half)
    keep = jnp.where(index > 0, 1.0, 0.0)
    for k in range(GROUPS):
        window[k] = window_tile(padded, space, k, half) * keep

    arrival.wait()

    def correct(k, carry):
        tile = window[k]
        for u in range(4):
            for p in range(16):
                even[4 * k + u + 1, p] = even[4 * k + u + 1, p] + tile
        return carry

    lax.fori_loop(NEAR // 4, GROUPS, correct, 0)
    run_sweeps(even, odd, scaled, fine.at[0], fine.at[1], fine.at[3], NEAR)
    (copy,) = move([(even.at[pl.ds(OWN + 1, 8)], result)], semaphores)
    means = restrict_own(even)
    after = jnp.minimum(index + 1, 15) * 8 + space
    changes = [(means[k] - own_end[k]) - received[after, k] for k in range(2)]
    for peer in range(128):
        for k in range(2):
            send[peer, k] = changes[k]
    copy.wait()


def finish(received, result, table, out, ends, padded, narrow, left, right, field, semaphores):
    half = half_mask()
    masks = edge_masks()
    index, space = coordinates()
    (copy,) = move([(result, field)], semaphores)
    difference_chain(received, 0, table, ends, masks, half)
    spread(padded, [ends[index, i] for i in range(16)], half)
    matrix = interleave_matrix(True)
    copy.wait()
    for k in range(2):
        tile = window_tile(padded, space, 8 + k, half)
        for i in range(4 * k, 4 * k + 4):
            for yi in range(4):
                for pair in range(2):
                    p = yi * 4 + 2 * pair
                    even, odd = field[i, p] + tile, field[i, p + 1] + tile
                    lanes = pl.ds(pair * 128, 128)
                    left[pl.ds(i * 32 + yi * 8, 8), lanes] = jnp.where(half, even, swap(odd))
                    left[pl.ds((15 - i) * 32 + yi * 8, 8), lanes] = jnp.where(
                        half, swap(even), odd
                    )
    right[...] = split_dot(left[...], matrix)
    for side in range(2):
        lanes = pl.ds(side * 128, 128)
        for plane in range(16):
            for yi in range(4):
                rows = pl.ds(plane * 32 + yi, 8, stride=4)
                narrow[side, rows, :] = right[pl.ds(plane * 32 + yi * 8, 8), lanes]
        out[0, :, :, lanes] = narrow[side].reshape(16, 32, 128)


def call(kernel, operands, results, scratch, copies=0, flops=0, vmem=VMEM):
    where = {
        "scalar": pltpu.SMEM, "near": pltpu.VMEM, "far": pltpu.HBM,
    }
    shapes = [jax.ShapeDtypeStruct(shape, f32) for shape, _ in results]
    arrays = [x for x, _ in operands]
    moved = sum(4 * x.size for x in arrays) + sum(4 * x.size for x in shapes)
    semaphores = [pltpu.SemaphoreType.DMA((copies,))] if copies else []
    return pl.pallas_call(
        kernel,
        out_shape=shapes,
        in_specs=[pl.BlockSpec(memory_space=where[w]) for _, w in operands],
        out_specs=[pl.BlockSpec(memory_space=where[w]) for _, w in results],
        scratch_shapes=[pltpu.VMEM(shape, f32) for shape in scratch] + semaphores,
        compiler_params=pltpu.CompilerParams(vmem_limit_bytes=vmem),
        cost_estimate=pl.CostEstimate(flops=flops, bytes_accessed=moved, transcendentals=0),
        name=kernel.__name__,
    )(*arrays)


def on_device(initial_temp, region_labels, region_rate, heat_rate):
    peers = lax.axis_size("space")
    tile = (8, 128)
    block_shape = (8, 16) + tile
    buffer = (WINDOW + 2, 16) + tile

    block, send, values = call(
        to_phases,
        [(region_rate, "scalar"), (heat_rate.T, "scalar"), (initial_temp, "near"), (region_labels, "near")],
        [(block_shape, "near"), ((8, 4) + tile, "near"), ((17 * REGIONS,) + tile, "near")],
        [(2, 512, 128), (512, 256), (512, 256)],
    )

    def beside(by, routes):
        pairs = [
            (t * peers + s + by, to * peers + s)
            for t, to in routes for s in range(peers) if 0 <= s + by < peers
        ]
        return lax.ppermute(block, ("tm", "space"), pairs)

    sides = [
        (beside(-1, ((8, 1), (10, 0))), "far"), (beside(1, ((9, 1), (11, 0))), "far"),
        (beside(-2, ((2, 1),)), "far"), (beside(2, ((6, 1),)), "far"),
    ]
    received = lax.all_to_all(
        send.reshape(8 * 32, 128), "space", 0, 0, tiled=True
    ).reshape((8, 4) + tile)

    base, fine, table, window = call(
        first_chain,
        [(values, "near"), (received, "near")],
        [((4,) + tile, "near"), ((4, GROUPS) + tile, "near"), ((3, 16) + tile, "near"),
         ((GROUPS,) + tile, "near")],
        [(17, 16) + tile, (48,) + tile],
    )
    base, fine, table, window = ((x, "near") for x in (base, fine, table, window))
    (send,) = call(
        first_sweeps,
        [(block, "far"), *sides, base, fine, window],
        [((128, 2) + tile, "near")],
        [buffer, buffer, buffer, (2,) + block_shape],
        copies=3,
    )

    def gather(array):
        rows = array.reshape(128 * 16, 128)
        rows = lax.all_to_all(rows, ("tm", "space"), 0, 0, tiled=True)
        return (rows.reshape((128, 2) + tile), "near")

    received = gather(send)
    (state,) = call(
        wide_sweeps,
        [fine, window, (block, "far"), *sides],
        [((WINDOW - NEAR, 16) + tile, "far")],
        [buffer, buffer, buffer, (4,) + block_shape],
        copies=5, flops=10**8, vmem=WIDE_VMEM,
    )
    send, result = call(
        second_sweeps,
        [received, (state, "far"), base, fine, table],
        [((128, 2) + tile, "near"), (block_shape, "far")],
        [(16, 16) + tile, (48,) + tile, buffer, buffer, buffer, (GROUPS,) + tile],
        copies=1,
    )
    (out,) = call(
        finish,
        [gather(send), (result, "far"), table],
        [((1, 16, 32, 256), "near")],
        [(16, 16) + tile, (48,) + tile, (2, 512, 128), (512, 256), (512, 256), block_shape],
        copies=1,
    )
    return out


def solution(mesh):
    return jax.shard_map(
        on_device,
        mesh=mesh,
        in_specs=(P("space", None, None), P("space", None, None), P(), P()),
        out_specs=P("tm", "space", None, None),
        check_vma=False,
    )
```

```python
import jax
import jax.numpy as jnp
from jax import lax
from jax.experimental import pallas as pl
from jax.experimental.pallas import tpu as pltpu
from jax.sharding import PartitionSpec as P


FINE_STEPS = 2
SWEEPS = 8
C_SWEEPS = 4
REGIONS = 6
WINDOW = 40
NEAR = 16
OWN = 32
GROUPS = WINDOW // 4
UNROLL = 8
VMEM = 24 * 1024 * 1024
WIDE_VMEM = 62 * 1024 * 1024

f32 = jnp.float32


def lane_of():
    return lax.broadcasted_iota(jnp.int32, (8, 128), 1)


def coordinates():
    return lax.axis_index("tm"), lax.axis_index("space")


def half_mask():
    return lane_of() < 64


def edge_masks():
    lane = lane_of()
    column = lax.rem(lane, 64)
    row = lax.broadcasted_iota(jnp.int32, (8, 128), 0)
    return row == 0, row == 7, column == 0, column == 63


def swap(tile):
    return pltpu.roll(tile, 64, 1)


def row_up(tile, masks):
    return jnp.where(masks[0], 0.0, pltpu.roll(tile, 1, 0))


def row_down(tile, masks):
    return jnp.where(masks[1], 0.0, pltpu.roll(tile, 7, 0))


def lane_up(tile, masks):
    return jnp.where(masks[2], 0.0, pltpu.roll(tile, 1, 1))


def lane_down(tile, masks):
    return jnp.where(masks[3], 0.0, pltpu.roll(tile, 127, 1))


def sweep(source, target, scaled, weight_ref, group, masks, fresh=None):
    def planes(base, last):
        for u in range(UNROLL):
            i = base + u + 1
            k = lax.shift_right_logical(base + u, 2)
            weight = weight_ref[k]
            if fresh is not None:
                inverse, heat = fresh[0][k], fresh[1][k]
            cur = [source[i, p] for p in range(16)]
            for p in range(16):
                yi, zi = p // 4, p % 4
                total = source[i - 1, p] + source[i + 1, p]
                above = cur[p - 4] if yi > 0 else row_up(cur[p + 12], masks)
                below = cur[p + 4] if yi < 3 else row_down(cur[p - 12], masks)
                left = cur[p - 1] if zi > 0 else lane_up(cur[p + 3], masks)
                right = cur[p + 1] if zi < 3 else lane_down(cur[p - 3], masks)
                total = total + ((above + below) + (left + right))
                if fresh is None:
                    term = scaled[i, p]
                else:
                    term = (cur[p] + heat) * inverse
                    scaled[i, p] = term
                value = term + weight * total
                target[i, p] = value
                if last and u == UNROLL - 1:
                    target[WINDOW + 1, p] = swap(value)

    def body(t, carry):
        planes(UNROLL * t, False)
        return carry

    lax.fori_loop(group, WINDOW // UNROLL - 1, body, 0)
    planes(jnp.int32(WINDOW - UNROLL), True)


def fold(buffer):
    for p in range(16):
        buffer[WINDOW + 1, p] = swap(buffer[WINDOW, p])


def run_sweeps(even, odd, scaled, inverse_ref, weight_ref, source_ref, first):
    masks = edge_masks()

    def one(source, target, q, fresh=None):
        group = lax.div(first + q, UNROLL)
        sweep(source, target, scaled, weight_ref, group, masks, fresh)

    fold(even)
    for step in range(FINE_STEPS):
        base = step * SWEEPS
        one(even, odd, jnp.int32(base + 1), (inverse_ref, source_ref))

        def pair(j, carry):
            one(odd, even, base + 2 * j + 2)
            one(even, odd, base + 2 * j + 3)
            return carry

        lax.fori_loop(0, SWEEPS // 2 - 1, pair, 0)
        one(odd, even, jnp.int32(base + SWEEPS))


def fill(buffer, tiles_ref, first, last):
    def body(k, carry):
        tile = tiles_ref[k]
        for u in range(4):
            for p in range(16):
                buffer[4 * k + u + 1, p] = tile
        return carry

    lax.fori_loop(first, last, body, 0)


def fill_sides(buffer, first, left, right):
    half = half_mask()

    def body(j, carry):
        for p in range(16):
            buffer[first + j + 1, p] = jnp.where(half, left[j, p], right[j, p])
            buffer[first + 16 - j, p] = swap(jnp.where(half, right[j, p], left[j, p]))
        return carry

    lax.fori_loop(0, 8, body, 0)


def restrict_own(buffer):
    tiles = []
    for k in range(2):
        parts = []
        for i in range(4):
            for p in range(16):
                tile = buffer[OWN + 4 * k + i + 1, p]
                if len(parts) < 8:
                    parts.append(tile)
                else:
                    parts[p % 8] = parts[p % 8] + tile
        while len(parts) > 1:
            parts = [parts[j] + parts[j + 1] for j in range(0, len(parts), 2)]
        tiles.append(parts[0] * (1.0 / 64.0))
    return tiles


def coarse_sweep(field, scaled, weight, masks):
    result = []
    for i in range(16):
        here = field[i]
        beyond = field[i + 1] if i < 15 else swap(here)
        total = (row_up(here, masks) + row_down(here, masks)) + (
            lane_up(here, masks) + lane_down(here, masks)
        )
        total = total + (beyond + field[i - 1] if i > 0 else beyond)
        result.append(scaled[i] + weight[i] * total)
    return result


def blocks_to_global(load, half):
    tiles = []
    for i in range(16):
        block, place = i // 4, i % 4
        if place < 2:
            tiles.append(jnp.where(half, load(block, place), load(7 - block, place)))
        else:
            tiles.append(
                swap(jnp.where(half, load(7 - block, 3 - place), load(block, 3 - place)))
            )
    return tiles


def spread(padded, tiles, half):
    for i in range(16):
        other = swap(tiles[i])
        padded[8 + i] = jnp.where(half, tiles[i], other)
        padded[39 - i] = jnp.where(half, other, tiles[i])


def window_tile(padded, space, k, half):
    return jnp.where(half, padded[4 * space + k], padded[4 * space + 19 - k])


def difference_chain(received, shift, table_ref, ends, masks, half):
    def arrived(sender):
        return blocks_to_global(lambda b, k: received[sender * 8 + b, k], half)

    def body(m, delta):
        scaled = [delta[i] * table_ref[0, i] for i in range(16)]
        weight = [table_ref[1, i] for i in range(16)]
        field = list(delta)
        for _ in range(C_SWEEPS):
            field = coarse_sweep(field, scaled, weight, masks)
        for i in range(16):
            ends[m, i] = field[i]
        added = arrived(jnp.minimum(m + shift, 15))
        return tuple(field[i] + added[i] for i in range(16))

    for i in range(16):
        ends[0, i] = jnp.zeros((8, 128), f32)
    lax.fori_loop(1, 16, body, tuple(arrived(shift)))


def split_dot(values, matrix):
    high = values.astype(jnp.bfloat16)
    rest = values - high.astype(f32)
    middle = rest.astype(jnp.bfloat16)
    low = (rest - middle.astype(f32)).astype(jnp.bfloat16)

    def dot(part):
        return jnp.dot(part, matrix, preferred_element_type=f32)

    return dot(high) + (dot(middle) + dot(low))


def interleave_matrix(transposed):
    rows = lax.broadcasted_iota(jnp.int32, (256, 256), 0)
    columns = lax.broadcasted_iota(jnp.int32, (256, 256), 1)
    z, c = (columns, rows) if transposed else (rows, columns)
    hit = z == 4 * lax.rem(c, 64) + lax.div(c, 64)
    return jnp.where(hit, 1.0, 0.0).astype(jnp.bfloat16)


def to_phases(initial, labels, block, send, narrow, left, right):
    half = half_mask()
    matrix = interleave_matrix(False)
    for side in range(2):
        lanes = pl.ds(side * 128, 128)
        narrow[side] = initial[:, :, lanes].reshape(512, 128)
        for plane in range(16):
            for yi in range(4):
                rows = pl.ds(plane * 32 + yi, 8, stride=4)
                left[pl.ds(plane * 32 + yi * 8, 8), lanes] = narrow[side, rows, :]
    right[...] = split_dot(left[...], matrix)
    sums = []
    for k in range(2):
        total = jnp.zeros((8, 128), f32)
        for i in range(4 * k, 4 * k + 4):
            for yi in range(4):
                for pair in range(2):
                    lanes = pl.ds(pair * 128, 128)
                    a = right[pl.ds(i * 32 + yi * 8, 8), lanes]
                    b = right[pl.ds((15 - i) * 32 + yi * 8, 8), lanes]
                    even = jnp.where(half, a, swap(b))
                    odd = jnp.where(half, swap(a), b)
                    block[i, yi * 4 + 2 * pair] = even
                    block[i, yi * 4 + 2 * pair + 1] = odd
                    total = total + (even + odd)
        sums.append(total * (1.0 / 64.0))
    tags = [
        jnp.concatenate([labels[k], labels[3 - k]], axis=1).astype(f32) for k in range(2)
    ]
    for peer in range(8):
        for k in range(2):
            send[peer, k] = sums[k]
            send[peer, 2 + k] = tags[k]


def regions(tags, values):
    total = jnp.where(tags == 0.0, values[0], 0.0)
    for region in range(1, len(values)):
        total = jnp.where(tags == region, values[region], total)
    return total


def first_chain(values, received, base, fine, table, window, chain, padded):
    half = half_mask()
    masks = edge_masks()
    index, space = coordinates()
    before = jnp.maximum(index - 1, 0)
    rate_values = [values[r] for r in range(REGIONS)]

    def heat_values(m):
        return [values[REGIONS * (m + 1) + r] for r in range(REGIONS)]

    tags = blocks_to_global(lambda b, k: received[b, 2 + k], half)
    start = blocks_to_global(lambda b, k: received[b, k], half)
    for i in range(16):
        rate = FINE_STEPS * regions(tags[i], rate_values) / 16.0
        inverse = 1.0 / (1.0 + 6.0 * rate)
        table[0, i] = inverse
        table[1, i] = rate * inverse
        table[2, i] = tags[i]
        chain[0, i] = start[i]

    outside = jnp.full((8, 128), -1.0, f32)
    for i in range(8):
        padded[i] = outside
        padded[40 + i] = outside
    spread(padded, tags, half)
    for k in range(GROUPS):
        tag = window_tile(padded, space, k, half)
        rate = regions(tag, rate_values)
        inverse = jnp.where(tag < 0.0, 0.0, 1.0 / (1.0 + 6.0 * rate))
        fine[0, k] = inverse
        fine[1, k] = rate * inverse
        fine[2, k] = regions(tag, heat_values(before))
        fine[3, k] = regions(tag, heat_values(index))

    def advance(m, state):
        heats = [FINE_STEPS * x for x in heat_values(m)]
        weight = [table[1, i] for i in range(16)]
        rows = [
            (state[i] + regions(table[2, i], heats)) * table[0, i] for i in range(16)
        ]
        field = list(state)
        for _ in range(C_SWEEPS):
            field = coarse_sweep(field, rows, weight, masks)
        for i in range(16):
            chain[m + 1, i] = field[i]
        return tuple(field)

    lax.fori_loop(0, 16, advance, tuple(start))

    nothing = jnp.zeros((8, 128), f32)
    for i in range(8):
        padded[i] = nothing
        padded[40 + i] = nothing
    spread(padded, [chain[before + 1, i] for i in range(16)], half)
    for k in range(2):
        base[k] = window_tile(padded, space, 8 + k, half)
    spread(padded, [chain[index + 1, i] for i in range(16)], half)
    for k in range(2):
        base[2 + k] = window_tile(padded, space, 8 + k, half)
    spread(padded, [chain[before, i] for i in range(16)], half)
    for k in range(GROUPS):
        window[k] = window_tile(padded, space, k, half)


def move(pairs, semaphores):
    copies = [
        pltpu.make_async_copy(source, target, semaphores.at[j])
        for j, (source, target) in enumerate(pairs)
    ]
    for copy in copies:
        copy.start()
    return copies


def move_now(pairs, semaphores):
    for copy in move(pairs, semaphores):
        copy.wait()


def first_sweeps(
    block, left, right, far_left, far_right, base, fine, window,
    send, even, odd, scaled, sides, semaphores,
):
    index, _ = coordinates()

    @pl.when(index >= 2)
    def _():
        fill(even, window, NEAR // 4, GROUPS)

    @pl.when(index < 2)
    def _():
        move_now(
            [(left, sides.at[0]), (right, sides.at[1]), (block, even.at[pl.ds(OWN + 1, 8)])],
            semaphores,
        )
        fill_sides(even, NEAR, sides.at[0], sides.at[1])

    run_sweeps(even, odd, scaled, fine.at[0], fine.at[1], fine.at[2], NEAR)
    means = restrict_own(even)
    for k in range(2):
        delta = means[k] - base[k]
        for peer in range(128):
            send[peer, k] = delta


def wide_sweeps(
    fine, window, block, left, right, far_left, far_right,
    state, even, odd, scaled, sides, semaphores,
):
    index, _ = coordinates()

    @pl.when(index < 2)
    def _():
        move_now(
            [(left, sides.at[0]), (right, sides.at[1]), (far_left, sides.at[2]),
             (far_right, sides.at[3]), (block, even.at[pl.ds(OWN + 1, 8)])],
            semaphores,
        )
        fill_sides(even, NEAR, sides.at[0], sides.at[1])
        fill_sides(even, 0, sides.at[2], sides.at[3])

    @pl.when(index >= 2)
    def _():
        fill(even, window, 0, GROUPS)

    @pl.when(index > 0)
    def _():
        run_sweeps(even, odd, scaled, fine.at[0], fine.at[1], fine.at[2], 0)

    move_now([(even.at[pl.ds(NEAR + 1, WINDOW - NEAR)], state)], semaphores.at[pl.ds(0, 1)])


def second_sweeps(
    received, state, base, fine, table,
    send, result,
    ends, padded, even, odd, scaled, window, semaphores,
):
    half = half_mask()
    masks = edge_masks()
    index, space = coordinates()
    (arrival,) = move([(state, even.at[pl.ds(NEAR + 1, WINDOW - NEAR)])], semaphores)
    before = jnp.maximum(index - 1, 0)
    difference_chain(received, 1, table, ends, masks, half)

    nothing = jnp.zeros((8, 128), f32)
    for i in range(8):
        padded[i] = nothing
        padded[40 + i] = nothing
    spread(padded, [ends[index, i] for i in range(16)], half)
    own_end = [window_tile(padded, space, 8 + k, half) + base[2 + k] for k in range(2)]
    spread(padded, [ends[before, i] for i in range(16)], half)
    keep = jnp.where(index > 0, 1.0, 0.0)
    for k in range(GROUPS):
        window[k] = window_tile(padded, space, k, half) * keep

    arrival.wait()

    def correct(k, carry):
        tile = window[k]
        for u in range(4):
            for p in range(16):
                even[4 * k + u + 1, p] = even[4 * k + u + 1, p] + tile
        return carry

    lax.fori_loop(NEAR // 4, GROUPS, correct, 0)
    run_sweeps(even, odd, scaled, fine.at[0], fine.at[1], fine.at[3], NEAR)
    (copy,) = move([(even.at[pl.ds(OWN + 1, 8)], result)], semaphores)
    means = restrict_own(even)
    after = jnp.minimum(index + 1, 15) * 8 + space
    changes = [(means[k] - own_end[k]) - received[after, k] for k in range(2)]
    for peer in range(128):
        for k in range(2):
            send[peer, k] = changes[k]
    copy.wait()


def finish(received, result, table, out, ends, padded, narrow, left, right, field, semaphores):
    half = half_mask()
    masks = edge_masks()
    index, space = coordinates()
    (copy,) = move([(result, field)], semaphores)
    difference_chain(received, 0, table, ends, masks, half)
    spread(padded, [ends[index, i] for i in range(16)], half)
    matrix = interleave_matrix(True)
    copy.wait()
    for k in range(2):
        tile = window_tile(padded, space, 8 + k, half)
        for i in range(4 * k, 4 * k + 4):
            for yi in range(4):
                for pair in range(2):
                    p = yi * 4 + 2 * pair
                    even, odd = field[i, p] + tile, field[i, p + 1] + tile
                    lanes = pl.ds(pair * 128, 128)
                    left[pl.ds(i * 32 + yi * 8, 8), lanes] = jnp.where(half, even, swap(odd))
                    left[pl.ds((15 - i) * 32 + yi * 8, 8), lanes] = jnp.where(
                        half, swap(even), odd
                    )
    right[...] = split_dot(left[...], matrix)
    for side in range(2):
        lanes = pl.ds(side * 128, 128)
        for plane in range(16):
            for yi in range(4):
                rows = pl.ds(plane * 32 + yi, 8, stride=4)
                narrow[side, rows, :] = right[pl.ds(plane * 32 + yi * 8, 8), lanes]
        out[0, :, :, lanes] = narrow[side].reshape(16, 32, 128)


def call(kernel, operands, results, scratch, copies=0, flops=0, vmem=VMEM):
    where = {
        "scalar": pltpu.SMEM, "near": pltpu.VMEM, "far": pltpu.HBM,
    }
    shapes = [jax.ShapeDtypeStruct(shape, f32) for shape, _ in results]
    arrays = [x for x, _ in operands]
    moved = sum(4 * x.size for x in arrays) + sum(4 * x.size for x in shapes)
    semaphores = [pltpu.SemaphoreType.DMA((copies,))] if copies else []
    return pl.pallas_call(
        kernel,
        out_shape=shapes,
        in_specs=[pl.BlockSpec(memory_space=where[w]) for _, w in operands],
        out_specs=[pl.BlockSpec(memory_space=where[w]) for _, w in results],
        scratch_shapes=[pltpu.VMEM(shape, f32) for shape in scratch] + semaphores,
        compiler_params=pltpu.CompilerParams(vmem_limit_bytes=vmem),
        cost_estimate=pl.CostEstimate(flops=flops, bytes_accessed=moved, transcendentals=0),
        name=kernel.__name__,
    )(*arrays)


def on_device(initial_temp, region_labels, region_rate, heat_rate):
    peers = lax.axis_size("space")
    tile = (8, 128)
    block_shape = (8, 16) + tile
    buffer = (WINDOW + 2, 16) + tile

    block, send = call(
        to_phases,
        [(initial_temp, "near"), (region_labels, "near")],
        [(block_shape, "near"), ((8, 4) + tile, "near")],
        [(2, 512, 128), (512, 256), (512, 256)],
    )

    def beside(by, routes):
        pairs = [
            (t * peers + s + by, to * peers + s)
            for t, to in routes for s in range(peers) if 0 <= s + by < peers
        ]
        return lax.ppermute(block, ("tm", "space"), pairs)

    sides = [
        (beside(-1, ((8, 1), (10, 0))), "far"), (beside(1, ((9, 1), (11, 0))), "far"),
        (beside(-2, ((2, 1),)), "far"), (beside(2, ((6, 1),)), "far"),
    ]
    received = lax.all_to_all(
        send.reshape(8 * 32, 128), "space", 0, 0, tiled=True
    ).reshape((8, 4) + tile)

    rows = jnp.concatenate([region_rate, heat_rate.reshape(-1)])
    values = jnp.broadcast_to(rows[:, None, None], (17 * REGIONS,) + tile)
    base, fine, table, window = call(
        first_chain,
        [(values, "near"), (received, "near")],
        [((4,) + tile, "near"), ((4, GROUPS) + tile, "near"), ((3, 16) + tile, "near"),
         ((GROUPS,) + tile, "near")],
        [(17, 16) + tile, (48,) + tile],
    )
    base, fine, table, window = ((x, "near") for x in (base, fine, table, window))
    (send,) = call(
        first_sweeps,
        [(block, "far"), *sides, base, fine, window],
        [((128, 2) + tile, "near")],
        [buffer, buffer, buffer, (2,) + block_shape],
        copies=3,
    )

    def gather(array):
        rows = array.reshape(128 * 16, 128)
        rows = lax.all_to_all(rows, ("tm", "space"), 0, 0, tiled=True)
        return (rows.reshape((128, 2) + tile), "near")

    received = gather(send)
    (state,) = call(
        wide_sweeps,
        [fine, window, (block, "far"), *sides],
        [((WINDOW - NEAR, 16) + tile, "far")],
        [buffer, buffer, buffer, (4,) + block_shape],
        copies=5, flops=10**8, vmem=WIDE_VMEM,
    )
    send, result = call(
        second_sweeps,
        [received, (state, "far"), base, fine, table],
        [((128, 2) + tile, "near"), (block_shape, "far")],
        [(16, 16) + tile, (48,) + tile, buffer, buffer, buffer, (GROUPS,) + tile],
        copies=1,
    )
    (out,) = call(
        finish,
        [gather(send), (result, "far"), table],
        [((1, 16, 32, 256), "near")],
        [(16, 16) + tile, (48,) + tile, (2, 512, 128), (512, 256), (512, 256), block_shape],
        copies=1,
    )
    return out


def solution(mesh):
    return jax.shard_map(
        on_device,
        mesh=mesh,
        in_specs=(P("space", None, None), P("space", None, None), P(), P()),
        out_specs=P("tm", "space", None, None),
        check_vma=False,
    )
```
